32 devices in a mesh: grp: 2 (over x), seq: 16 (over z, y, core).
Axes of the slice: x: 2, y: 2, z: 4, core: 2. Of those that a mesh axis runs over, the one named last changes fastest.
Arguments:
- query_inputs: bfloat16 [32768, 128], P(('grp', 'seq')), parts along dimension 0, may hold values from -6 to 6
- key_inputs: bfloat16 [32768, 128], P(('grp', 'seq')), parts along dimension 0, may hold values from -5.3 to 4.8
- value_inputs: bfloat16 [32768, 2048], P(('grp', 'seq')), parts along dimension 0, may hold values from -5.3 to 4.8
- log_decay: float32 [16, 32768], P(None, ('grp', 'seq')), parts along dimension 1, may hold values from -0.9 to 0, as said below
- level_weight: bfloat16 [15, 16, 32768], P(None, None, ('grp', 'seq')), parts along dimension 2, may hold values from 0.099609375 to 1
- conv_weight: float32 [4, 2304], replicated, may hold values from 0.35 to 0.65
- norm_gain: float32 [2048], replicated, may hold values from 0.1 to 1.9
Outputs:
- mixer_out: bfloat16 [32768, 2048], P(('grp', 'seq')), parts along dimension 0
The draws below stay inside these ranges and needn't reach their ends.
There are 2 independent parts, one for each index of `grp`. The reference program is written for one: setup_inputs(seed, part) draws one part's arguments, and reference() takes and returns one part's arrays. A program takes and returns all parts, laid end to end along the dimension named above; an argument that names none is the same for every part. Nothing has to cross between parts.
Inputs may be any that keep to these rules, and one draw needn't show every extreme that they name: `log_decay`: each entry is the logarithm of one head's decay factor at one token.
All inputs are finite; a program needn't handle non-finite values.
Results may differ from the reference program's by a relative error of at most 0.014.
Values may be sent and summed in bfloat16 or wider, within the bound.
A program may use at most 64 MiB of HBM per device.

```python
import math
import jax
import jax.numpy as jnp
import numpy as np
from jax import lax

HEAD_TOTAL = 16
HEAD_DIM = 128
STATE = 128
KERNEL = 4
TOK_DEV = 1024
LOG_TOK = 10
LOG_SEQ = 4
LEVELS = 15
TOKEN_TOTAL = 16384
N_SEQ = 16


def draw_log_decay(key, part):
    random_subkeys = jax.random.split(key, 8)
    keep_share = 0.5
    middle_share = 0.25
    shard_count = TOKEN_TOTAL // TOK_DEV
    shard_ordinal = jax.random.permutation(random_subkeys[0], HEAD_TOTAL).astype(jnp.float32)
    keeper = shard_ordinal < HEAD_TOTAL * keep_share
    middle = jnp.logical_and(jnp.logical_not(keeper), shard_ordinal < HEAD_TOTAL * (keep_share + middle_share))
    quick_decay_heads = jnp.logical_and(jnp.logical_not(keeper), jnp.logical_not(middle))
    fast_rate = jnp.exp(jax.random.uniform(random_subkeys[1], (HEAD_TOTAL,), jnp.float32, math.log(0.06), math.log(0.15)))
    keep_rate = jnp.exp(jax.random.uniform(random_subkeys[2], (HEAD_TOTAL,), jnp.float32, math.log(0.15 / TOKEN_TOTAL), math.log(0.75 / TOKEN_TOTAL)))
    middle_rate = jnp.exp(jax.random.uniform(random_subkeys[7], (HEAD_TOTAL,), jnp.float32, math.log(0.15 / TOK_DEV), math.log(1.5 / TOK_DEV)))
    head_decay_rate = jnp.where(keeper, keep_rate, jnp.where(middle, middle_rate, fast_rate))
    shard_factor = jnp.exp(jax.random.uniform(random_subkeys[3], (HEAD_TOTAL, shard_count, 1), jnp.float32, -0.7, 0.7))
    token_factor = jnp.exp(jax.random.uniform(random_subkeys[4], (HEAD_TOTAL, shard_count, TOK_DEV), jnp.float32, -0.7, 0.7))
    growth_multiplier = (shard_factor * token_factor).reshape(HEAD_TOTAL, TOKEN_TOTAL)
    span_start_positions = jax.random.randint(random_subkeys[5], (2, HEAD_TOTAL), 0, TOKEN_TOTAL)
    sampled_span_lengths = jnp.log(1.0 - jax.random.uniform(random_subkeys[6], (2, HEAD_TOTAL), jnp.float32, 0.2, 0.5))
    leading_row = jnp.where(shard_ordinal == 0.0, math.log(0.4), sampled_span_lengths[0])
    span_lengths = jnp.stack([leading_row, sampled_span_lengths[1]], axis=0)
    position_list = jnp.arange(TOKEN_TOTAL, dtype=jnp.int32)
    token_spans = jnp.zeros((HEAD_TOTAL, TOKEN_TOTAL), jnp.float32)
    for span_position in range(2):
        token_spans = token_spans + jnp.where(position_list[None, :] == span_start_positions[span_position][:, None], span_lengths[span_position][:, None], 0.0)
    token_spans = jnp.where(quick_decay_heads[:, None], 0.0, token_spans)
    return jnp.maximum(-(head_decay_rate[:, None] * growth_multiplier) + token_spans, -0.9)


def centred_inputs(key, column_count):
    random_part = jnp.clip(jax.random.normal(key, (TOKEN_TOTAL, column_count), jnp.float32), -5.0, 5.0)
    return (random_part - 0.255).astype(jnp.bfloat16)


def draw_key_inputs(key, part):
    return centred_inputs(jax.random.fold_in(key, 17), STATE)


def draw_value_inputs(key, part):
    return centred_inputs(jax.random.fold_in(key, 29), HEAD_TOTAL * HEAD_DIM)


def draw_conv_weight(key, part):
    return jax.random.uniform(jax.random.fold_in(key, 41), (KERNEL, 2 * STATE + HEAD_TOTAL * HEAD_DIM), jnp.float32, 0.35, 0.65)


def block_levels(key, dims, cuts, least, top_value):
    loudness, own = 1.0, jax.random.fold_in(key, 6)
    for axis_at, blocks in cuts:
        heights = jnp.exp(jax.random.uniform(jax.random.fold_in(own, axis_at), (blocks,), jnp.float32, least / len(cuts), top_value / len(cuts)))
        loudness = loudness * jnp.repeat(heights, dims[axis_at] // blocks).reshape([-1 if axis == axis_at else 1 for axis in range(len(dims))])
    return loudness


def centred(own_key, extent, spread, reach, cuts=(), kind=jnp.bfloat16):
    level = block_levels(own_key, extent, cuts, -0.22, 0.18) if cuts else 1.0
    drawn = jax.random.normal(own_key, extent, jnp.float32) * spread * level
    return jnp.minimum(jnp.maximum(drawn, -reach), reach).astype(kind)


def setup_inputs(seed: int = 0, part: int = 0) -> dict:
    seeds = jax.random.split(jax.random.key(seed), 8)
    part_keys = jax.random.split(jax.random.fold_in(seeds[7], part), 8)
    query_inputs = centred(part_keys[0], (TOKEN_TOTAL, STATE), 1.0, 6.0, ((0, 16),))
    key_inputs = draw_key_inputs(jax.random.fold_in(jax.random.fold_in(seeds[7], part), 71), part)
    value_inputs = draw_value_inputs(jax.random.fold_in(jax.random.fold_in(seeds[7], part), 71), part)
    log_decay = draw_log_decay(jax.random.fold_in(jax.random.fold_in(seeds[7], part), 71), part)
    level_weight = jnp.clip(jnp.exp(math.log(1.0) - 2.306499 * jax.random.uniform(part_keys[4], (LEVELS, HEAD_TOTAL, TOKEN_TOTAL), jnp.float32) ** block_levels(part_keys[4], (LEVELS, HEAD_TOTAL, TOKEN_TOTAL), ((2, 16),), -0.2, 0.2)), 0.099609375, 1.0).astype(jnp.bfloat16)
    conv_weight = draw_conv_weight(jax.random.fold_in(seeds[7], 71), part)
    norm_gain = jnp.clip(1.0 + 0.18 * jax.random.normal(seeds[6], (HEAD_TOTAL * HEAD_DIM,), jnp.float32), 0.1, 1.9)
    return {"query_inputs": query_inputs, "key_inputs": key_inputs, "value_inputs": value_inputs, "log_decay": log_decay, "level_weight": level_weight, "conv_weight": conv_weight, "norm_gain": norm_gain}


EPSILON = 1e-05

def causal_conv(inputs, weight):
    tap_count = weight.shape[0]
    length = inputs.shape[0]
    padded = jnp.concatenate([jnp.zeros((tap_count - 1, inputs.shape[1]), inputs.dtype), inputs], axis=0).astype(jnp.float32)
    summed = jnp.zeros(inputs.shape, jnp.float32)
    for tap_pos in range(tap_count):
        summed = summed + weight[tap_pos][None, :] * padded[tap_pos:tap_pos + length]
    return jax.nn.silu(summed).astype(jnp.bfloat16)

def reference(query_inputs, key_inputs, value_inputs, log_decay, level_weight, conv_weight, norm_gain):
    queries = causal_conv(query_inputs, conv_weight[:, :STATE])
    keys_conv = causal_conv(key_inputs, conv_weight[:, STATE:2 * STATE])
    values_conv = causal_conv(value_inputs, conv_weight[:, 2 * STATE:])
    cumul_decay = jnp.cumsum(log_decay.reshape(HEAD_TOTAL, N_SEQ, TOK_DEV), axis=2)
    cumul_shards = jnp.transpose(cumul_decay, (1, 0, 2))
    query_shards = queries.reshape(N_SEQ, TOK_DEV, STATE)
    key_shards = keys_conv.reshape(N_SEQ, TOK_DEV, STATE)
    value_shards = values_conv.reshape(N_SEQ, TOK_DEV, HEAD_TOTAL, HEAD_DIM)
    weight_shards = jnp.transpose(level_weight.reshape(LEVELS, HEAD_TOTAL, N_SEQ, TOK_DEV), (2, 0, 1, 3))

    def group_of(inputs):
        key_rows, value_rows, cumul_rows = inputs
        tail_decay = jnp.exp(cumul_rows[:, TOK_DEV - 1:] - cumul_rows)
        decayed = (key_rows.astype(jnp.float32)[None, :, :] * tail_decay[:, :, None]).astype(jnp.bfloat16)
        return jnp.einsum('hcn,chp->hnp', decayed.astype(jnp.float32), value_rows.astype(jnp.float32))
    group_state = lax.map(group_of, (key_shards, value_shards, cumul_shards))
    shard_ids = np.arange(N_SEQ)
    block_state = group_state
    block_total = cumul_shards[:, :, TOK_DEV - 1]
    offset = jnp.zeros_like(block_total)
    buckets = []
    for bit_pos in range(LOG_SEQ):
        partner = jnp.asarray((shard_ids ^ 1 << bit_pos).astype(np.int32))
        other_state = block_state[partner]
        other_total = block_total[partner]
        upper_half = shard_ids >> bit_pos & 1 == 1
        upper_state = upper_half[:, None, None, None]
        lifted = jnp.exp(offset)[:, :, None, None] * other_state
        buckets.append(jnp.where(upper_state, lifted, 0.0).astype(jnp.bfloat16))
        block_state = jnp.where(upper_state, block_state + jnp.exp(block_total)[:, :, None, None] * other_state, other_state + jnp.exp(other_total)[:, :, None, None] * block_state)
        block_total = block_total + other_total
        offset = offset + jnp.where(upper_half[:, None], other_total, 0.0)
    bucket_all = jnp.stack(buckets, axis=1)

    def shard_out(inputs):
        query_rows, key_rows, value_rows, cumul_rows, weight_rows, bucket_rows = inputs
        scores = jnp.dot(query_rows, key_rows.T, preferred_element_type=jnp.float32)
        position_list = jnp.arange(TOK_DEV, dtype=jnp.int32)
        differ = jnp.bitwise_xor(position_list[:, None], position_list[None, :])
        levels = jnp.zeros((TOK_DEV, TOK_DEV), jnp.int32)
        for bit_pos in range(LOG_TOK):
            levels = levels + (differ >= 1 << bit_pos).astype(jnp.int32)
        causal = position_list[:, None] >= position_list[None, :]
        query_float = query_rows.astype(jnp.float32)

        def head_out(head_idx):
            decay_row = cumul_rows[head_idx]
            weights_row = weight_rows[:, head_idx].astype(jnp.float32)
            mixing = jnp.zeros((TOK_DEV, TOK_DEV), jnp.float32)
            for level_pos in range(LOG_TOK + 1):
                mixing = mixing + jnp.where(levels == level_pos, weights_row[level_pos][:, None], 0.0)
            decay_gap = jnp.where(causal, decay_row[:, None] - decay_row[None, :], -1e+30)
            near_weight = (scores * mixing * jnp.exp(decay_gap)).astype(jnp.bfloat16)
            near_term = jnp.dot(near_weight, value_rows[:, head_idx], preferred_element_type=jnp.float32)
            far_scale = weights_row[LOG_TOK + 1:] * jnp.exp(decay_row)[None, :]
            far_query = (query_float[:, None, :] * far_scale.T[:, :, None]).astype(jnp.bfloat16).reshape(TOK_DEV, LOG_SEQ * STATE)
            head_buckets = bucket_rows[:, head_idx].reshape(LOG_SEQ * STATE, HEAD_DIM)
            pre_norm = near_term + jnp.dot(far_query, head_buckets, preferred_element_type=jnp.float32)
            gain_row = lax.dynamic_slice_in_dim(norm_gain, head_idx * HEAD_DIM, HEAD_DIM)
            normed = pre_norm * lax.rsqrt(lax.optimization_barrier(jnp.mean(pre_norm * pre_norm, axis=1, keepdims=True)) + EPSILON) * gain_row[None, :]
            return normed.astype(jnp.bfloat16)
        per_head = lax.map(head_out, jnp.arange(HEAD_TOTAL, dtype=jnp.int32))
        return jnp.transpose(per_head, (1, 0, 2)).reshape(TOK_DEV, HEAD_TOTAL * HEAD_DIM)
    shard_outputs = lax.map(shard_out, (query_shards, key_shards, value_shards, cumul_shards, weight_shards, bucket_all))
    return shard_outputs.reshape(TOKEN_TOTAL, HEAD_TOTAL * HEAD_DIM)
```

```python
import functools

import jax
import jax.numpy as jnp
from jax import lax
from jax.experimental import pallas as pl
from jax.experimental.pallas import tpu as pltpu
from jax.sharding import PartitionSpec as P

EPSILON = 1e-05
TILE = 128
SUB = 8
GROUP = 2
BF16 = jnp.bfloat16
F32 = jnp.float32
VMEM_BYTES = 40 * 1024 * 1024


def bits_of(number):
    return number.bit_length() - 1


def dot(a, b):
    return jnp.dot(a, b, preferred_element_type=F32)


def scaled(x, row):
    return x * row.astype(BF16)


def conv_tile(padded, weight, row, column, width):
    taps = weight.shape[0]
    first = SUB - taps + 1 + row
    total = None
    for tap in range(taps):
        term = padded[first + tap : first + tap + TILE, column : column + width] * weight[
            tap : tap + 1, column : column + width
        ]
        total = term if total is None else total + term
    half = total * 0.5
    return half + half * jnp.tanh(half)


def fill(padded, rim, current, column):
    rows, width = current.shape
    rim_rows = rim.shape[0]
    padded[SUB - rim_rows : SUB, column : column + width] = rim.astype(F32)
    padded[SUB : SUB + rows, column : column + width] = current.astype(F32)


def spread(cumul, places, width):
    heads = cumul.shape[0]
    return jnp.concatenate(
        [jnp.broadcast_to(cumul[:, at : at + 1], (heads, width)) for at in places], axis=1
    )


def tables(decay, level_weight, table, length, near_count):
    def put(index, value):
        for head in range(value.shape[0]):
            table[head, index : index + 1, :] = value[head : head + 1, :]

    lane = lax.broadcasted_iota(jnp.int32, decay.shape, 1)
    cumul = decay
    step = 1
    while step < length:
        cumul = cumul + jnp.where(lane >= step, pltpu.roll(cumul, step, 1), 0.0)
        step *= 2
    centre = spread(cumul, [at + TILE // 2 for at in range(0, length, TILE)], TILE)
    rise = jnp.exp(cumul - centre)
    put(0, jnp.exp(centre - cumul))
    tile_bits = bits_of(TILE)
    for level in range(tile_bits + 1):
        put(1 + level, level_weight[level].astype(F32) * rise)
    for level in range(tile_bits + 1, near_count):
        half = 1 << (level - 1)
        edge = spread(cumul, [at + half - 1 for at in range(0, length, 2 * half)], 2 * half)
        gap = cumul - edge
        upper = (lane & half) != 0
        fade = jnp.exp(jnp.where(upper, gap, -gap))
        put(1 + level, jnp.where(upper, level_weight[level].astype(F32), 1.0) * fade)
    fall = jnp.exp(cumul)
    for level in range(near_count, level_weight.shape[0]):
        put(1 + level, level_weight[level].astype(F32) * fall)
    put(1 + level_weight.shape[0], jnp.exp(cumul[:, length - 1 :] - cumul))


def prepare_kernel(
    near_count,
    query_in,
    key_in,
    value_in,
    rim_first,
    rim,
    weight_first,
    weight,
    decay,
    level_weight,
    query_turned,
    key_out,
    value_turned,
    table,
    state,
    padded,
):
    step = pl.program_id(0)
    length = query_in.shape[0]
    width = query_in.shape[1]
    group = state.shape[0]

    @pl.when(step == 0)
    def _():
        tables(decay[...], level_weight, table, length, near_count)
        fill(padded, rim_first[:, :width], query_in[...], 0)
        fill(padded, rim_first[:, width:], key_in[...], width)
        for row in range(0, length, TILE):
            query_tile = conv_tile(padded, weight_first, row, 0, width)
            query_turned[:, row : row + TILE] = query_tile.T.astype(BF16)
            key_tile = conv_tile(padded, weight_first, row, width, width)
            key_out[row : row + TILE, :] = key_tile.astype(BF16)

    fill(padded, rim[...], value_in[...], 0)
    tail_at = level_weight.shape[0] + 1
    head_width = state.shape[1]
    for own in range(group):
        at = own * head_width
        for row in range(0, length, TILE):
            tile = conv_tile(padded, weight, row, at, head_width)
            value_turned[at : at + head_width, row : row + TILE] = tile.T.astype(BF16)
        tail = table[step * group + own, tail_at : tail_at + 1, :]
        state[own] = dot(scaled(value_turned[at : at + head_width, :], tail), key_out[...])


def near_kernel(
    near_count, query_turned, key, value_turned, table, *rest
):
    near, scores = rest[-2:]
    step = pl.program_id(0)
    length = key.shape[0]
    tile_bits = bits_of(TILE)
    sub_bits = bits_of(SUB)

    @pl.when(step == 0)
    def _():
        for at in range(0, length, TILE):
            scores[at : at + TILE, :] = dot(
                key[at : at + TILE, :], query_turned[:, at : at + TILE]
            )

    def row_of(index, start, size):
        return table[0, index : index + 1, start : start + size]

    mid_states = {}
    for level in range(tile_bits + 1, near_count):
        half = 1 << (level - 1)
        for start in range(0, length, 2 * half):
            faded = scaled(value_turned[:, start : start + half], row_of(1 + level, start, half))
            mid_states[level, start] = dot(faded, key[start : start + half, :]).astype(BF16)

    sub_row = lax.broadcasted_iota(jnp.int32, (SUB, TILE), 0)
    sub_lane = lax.broadcasted_iota(jnp.int32, (SUB, TILE), 1)
    inner = sub_lane & (SUB - 1)
    inner_differ = inner ^ sub_row
    inner_causal = inner >= sub_row
    tile_of_lane = sub_lane >> sub_bits
    counts = TILE // SUB
    outer_row = lax.broadcasted_iota(jnp.int32, (counts, TILE), 0)
    outer = lax.broadcasted_iota(jnp.int32, (counts, TILE), 1) >> sub_bits
    outer_differ = outer ^ outer_row
    outer_causal = outer > outer_row

    for at in range(0, length, TILE):
        diagonal = jnp.broadcast_to(row_of(1, at, TILE), (SUB, TILE))
        for level in range(1, sub_bits + 1):
            diagonal = jnp.where(
                inner_differ >= 1 << (level - 1), row_of(1 + level, at, TILE), diagonal
            )
        diagonal = jnp.where(inner_causal, diagonal, 0.0)
        beside = jnp.broadcast_to(row_of(2 + sub_bits, at, TILE), (counts, TILE))
        for level in range(sub_bits + 2, tile_bits + 1):
            beside = jnp.where(
                outer_differ >= 1 << (level - sub_bits - 1), row_of(1 + level, at, TILE), beside
            )
        beside = jnp.where(outer_causal, beside, 0.0)
        mixing = jnp.concatenate(
            [
                jnp.where(
                    tile_of_lane == tile,
                    diagonal,
                    jnp.broadcast_to(beside[tile : tile + 1, :], (SUB, TILE)),
                )
                for tile in range(counts)
            ],
            axis=0,
        )
        left = [scaled(value_turned[:, at : at + TILE], row_of(0, at, TILE))]
        right = [(scores[at : at + TILE, :] * mixing).astype(BF16)]
        for level in range(tile_bits + 1, near_count):
            half = 1 << (level - 1)
            if at & half:
                left.append(mid_states[level, at // (2 * half) * (2 * half)])
                right.append(
                    scaled(query_turned[:, at : at + TILE], row_of(1 + level, at, TILE))
                )
        near[:, at : at + TILE] = dot(
            jnp.concatenate(left, axis=1), jnp.concatenate(right, axis=0)
        ).astype(BF16)


def far_kernel(near_count, query_turned, table, near, bucket, gain, output):
    length = query_turned.shape[1]
    seq_bits, group, head_width = bucket.shape[:3]
    span = 2 * TILE
    for own in range(group):
        at = own * head_width
        states = jnp.concatenate([bucket[j, own] for j in range(seq_bits)], axis=1)
        for start in range(0, length, span):
            queries = query_turned[:, start : start + span]
            far = jnp.concatenate(
                [
                    scaled(queries, table[own, 1 + near_count + j : 2 + near_count + j, start : start + span])
                    for j in range(seq_bits)
                ],
                axis=0,
            )
            total = dot(states, far) + near[at : at + head_width, start : start + span].astype(F32)
            power = jnp.mean(total * total, axis=0, keepdims=True)
            normed = total * lax.rsqrt(power + EPSILON)
            output[start : start + span, at : at + head_width] = (
                normed.T * gain[:, at : at + head_width]
            ).astype(BF16)


def whole(shape):
    return pl.BlockSpec(shape, lambda i: (0,) * len(shape))


def climb(state, totals, shard_index, seq_bits):
    size = totals.shape[0]
    shards = lax.iota(jnp.int32, size)
    block = state
    buckets = []
    for bit in range(seq_bits):
        pairs = [(i, i ^ 1 << bit) for i in range(size)]
        other = lax.ppermute(block.astype(BF16), "seq", pairs).astype(F32)
        upper = (shard_index >> bit & 1) == 1
        base = shard_index >> bit << bit
        top = (shard_index >> bit | 1) << bit
        before = jnp.logical_and(shards >= base, shards < shard_index)
        in_upper = jnp.logical_and(shards >= top, shards < top + (1 << bit))
        offset = jnp.sum(jnp.where(before[:, None], totals, 0.0), axis=0)
        lift = jnp.where(upper, jnp.exp(offset), 0.0)
        buckets.append((lift[:, None, None] * other).astype(BF16))
        if bit + 1 < seq_bits:
            fade = jnp.exp(jnp.sum(jnp.where(in_upper[:, None], totals, 0.0), axis=0))
            block = (
                jnp.where(upper, 1.0, fade)[:, None, None] * block
                + jnp.where(upper, fade, 1.0)[:, None, None] * other
            )
    return jnp.stack(buckets, axis=0)


def on_device(
    query_inputs, key_inputs, value_inputs, log_decay, level_weight, conv_weight, norm_gain
):
    length, width = query_inputs.shape
    channels = value_inputs.shape[1]
    heads = log_decay.shape[0]
    head_width = channels // heads
    taps = conv_weight.shape[0]
    levels = level_weight.shape[0]
    size = lax.axis_size("seq")
    seq_bits = bits_of(size)
    near_count = levels - seq_bits
    shard_index = lax.axis_index("seq")
    rim = jnp.concatenate(
        [x[length - taps + 1 :] for x in (query_inputs, key_inputs, value_inputs)], axis=1
    )
    rim = lax.ppermute(rim, "seq", [(i, i + 1) for i in range(size - 1)])
    totals = lax.all_gather(jnp.sum(log_decay, axis=1), "seq")

    group_width = GROUP * head_width
    table_count = levels + 2
    params = pltpu.CompilerParams(vmem_limit_bytes=VMEM_BYTES)
    query_turned, key, value_turned, table, state = pl.pallas_call(
        functools.partial(prepare_kernel, near_count),
        grid=(heads // GROUP,),
        in_specs=[
            whole((length, width)),
            whole((length, width)),
            pl.BlockSpec((length, group_width), lambda i: (0, i)),
            pl.BlockSpec((taps - 1, 2 * width), lambda i: (0, 0)),
            pl.BlockSpec((taps - 1, group_width), lambda i: (0, i + 2 * width // group_width)),
            pl.BlockSpec((taps, 2 * width), lambda i: (0, 0)),
            pl.BlockSpec((taps, group_width), lambda i: (0, i + 2 * width // group_width)),
            whole((heads, length)),
            whole((levels, heads, length)),
        ],
        out_specs=[
            whole((width, length)),
            whole((length, width)),
            pl.BlockSpec((group_width, length), lambda i: (i, 0)),
            whole((heads, table_count, length)),
            pl.BlockSpec((GROUP, head_width, width), lambda i: (i, 0, 0)),
        ],
        out_shape=[
            jax.ShapeDtypeStruct((width, length), BF16),
            jax.ShapeDtypeStruct((length, width), BF16),
            jax.ShapeDtypeStruct((channels, length), BF16),
            jax.ShapeDtypeStruct((heads, table_count, length), F32),
            jax.ShapeDtypeStruct((heads, head_width, width), F32),
        ],
        scratch_shapes=[pltpu.VMEM((SUB + length, max(group_width, 2 * width)), F32)],
        compiler_params=params,
        name="prepare",
    )(
        query_inputs,
        key_inputs,
        value_inputs,
        rim,
        rim,
        conv_weight,
        conv_weight,
        log_decay,
        level_weight,
    )

    pieces = min(seq_bits, 4)
    piece_heads = heads // pieces
    near = None
    for piece in range(pieces):
        first = piece * piece_heads
        chained = [] if near is None else [near]
        near = pl.pallas_call(
            functools.partial(near_kernel, near_count),
            grid=(piece_heads,),
            in_specs=[
                whole((width, length)),
                whole((length, width)),
                pl.BlockSpec((head_width, length), lambda i, first=first: (i + first, 0)),
                pl.BlockSpec((1, table_count, length), lambda i, first=first: (i + first, 0, 0)),
            ]
            + [pl.BlockSpec(memory_space=pl.ANY)] * len(chained),
            out_specs=pl.BlockSpec((head_width, length), lambda i, first=first: (i + first, 0)),
            out_shape=jax.ShapeDtypeStruct((channels, length), BF16),
            input_output_aliases={4: 0} if chained else {},
            scratch_shapes=[pltpu.VMEM((length, TILE), F32)],
            compiler_params=params,
            cost_estimate=pl.CostEstimate(
                flops=piece_heads * 2 * length * head_width * 8 * TILE * 4,
                bytes_accessed=4 * piece_heads * head_width * length,
                transcendentals=0,
            ),
            name="near",
        )(query_turned, key, value_turned, table, *chained)

    buckets = climb(state, totals, shard_index, seq_bits)
    return pl.pallas_call(
        functools.partial(far_kernel, near_count),
        grid=(heads // GROUP,),
        in_specs=[
            whole((width, length)),
            pl.BlockSpec((GROUP, table_count, length), lambda i: (i, 0, 0)),
            pl.BlockSpec((group_width, length), lambda i: (i, 0)),
            pl.BlockSpec((seq_bits, GROUP, head_width, width), lambda i: (0, i, 0, 0)),
            pl.BlockSpec((1, group_width), lambda i: (0, i)),
        ],
        out_specs=pl.BlockSpec((length, group_width), lambda i: (0, i)),
        out_shape=jax.ShapeDtypeStruct((length, channels), BF16),
        compiler_params=params,
        name="far",
    )(query_turned, table, near, buckets, norm_gain[None, :])


def solution(mesh):
    return jax.shard_map(
        on_device,
        mesh=mesh,
        in_specs=(
            P(("grp", "seq"), None),
            P(("grp", "seq"), None),
            P(("grp", "seq"), None),
            P(None, ("grp", "seq")),
            P(None, None, ("grp", "seq")),
            P(),
            P(),
        ),
        out_specs=P(("grp", "seq"), None),
        check_vma=False,
    )
```

```python
import functools

import jax
import jax.numpy as jnp
from jax import lax
from jax.experimental import pallas as pl
from jax.experimental.pallas import tpu as pltpu
from jax.sharding import PartitionSpec as P

EPSILON = 1e-05
TILE = 128
SUB = 8
GROUP = 2
BF16 = jnp.bfloat16
F32 = jnp.float32
MIB = 1024 * 1024


def bits_of(number):
    return number.bit_length() - 1


def dot(a, b):
    return jnp.dot(a, b, preferred_element_type=F32)


def scaled(x, row):
    return x * row.astype(BF16)


def conv_tile(padded, weight, row, column, width):
    taps = weight.shape[0]
    first = SUB - taps + 1 + row
    total = None
    for tap in range(taps):
        term = padded[first + tap : first + tap + TILE, column : column + width] * weight[
            tap : tap + 1, column : column + width
        ]
        total = term if total is None else total + term
    half = total * 0.5
    return half + half * jnp.tanh(half)


def fill(padded, rim, current, column):
    rows, width = current.shape
    rim_rows = rim.shape[0]
    padded[SUB - rim_rows : SUB, column : column + width] = rim.astype(F32)
    padded[SUB : SUB + rows, column : column + width] = current.astype(F32)


def spread(cumul, places, width):
    heads = cumul.shape[0]
    return jnp.concatenate(
        [jnp.broadcast_to(cumul[:, at : at + 1], (heads, width)) for at in places], axis=1
    )


def tables(decay, level_weight, table, length, near_count):
    def put(index, value):
        for head in range(value.shape[0]):
            table[head, index : index + 1, :] = value[head : head + 1, :]

    lane = lax.broadcasted_iota(jnp.int32, decay.shape, 1)
    cumul = decay
    step = 1
    while step < length:
        cumul = cumul + jnp.where(lane >= step, pltpu.roll(cumul, step, 1), 0.0)
        step *= 2
    centre = spread(cumul, [at + TILE // 2 for at in range(0, length, TILE)], TILE)
    rise = jnp.exp(cumul - centre)
    put(0, jnp.exp(centre - cumul))
    tile_bits = bits_of(TILE)
    for level in range(tile_bits + 1):
        put(1 + level, level_weight[level].astype(F32) * rise)
    for level in range(tile_bits + 1, near_count):
        half = 1 << (level - 1)
        edge = spread(cumul, [at + half - 1 for at in range(0, length, 2 * half)], 2 * half)
        gap = cumul - edge
        upper = (lane & half) != 0
        fade = jnp.exp(jnp.where(upper, gap, -gap))
        put(1 + level, jnp.where(upper, level_weight[level].astype(F32), 1.0) * fade)
    fall = jnp.exp(cumul)
    for level in range(near_count, level_weight.shape[0]):
        put(1 + level, level_weight[level].astype(F32) * fall)
    put(1 + level_weight.shape[0], jnp.exp(cumul[:, length - 1 :] - cumul))


def prepare_kernel(
    near_count,
    query_in,
    key_in,
    value_in,
    rim_first,
    rim,
    weight_first,
    weight,
    decay,
    level_weight,
    query_turned,
    key_out,
    value_turned,
    table,
    state,
    padded,
):
    step = pl.program_id(0)
    length = query_in.shape[0]
    width = query_in.shape[1]
    group = state.shape[0]

    @pl.when(step == 0)
    def _():
        tables(decay[...], level_weight, table, length, near_count)
        fill(padded, rim_first[:, :width], query_in[...], 0)
        fill(padded, rim_first[:, width:], key_in[...], width)
        for row in range(0, length, TILE):
            query_tile = conv_tile(padded, weight_first, row, 0, width)
            query_turned[:, row : row + TILE] = query_tile.T.astype(BF16)
            key_tile = conv_tile(padded, weight_first, row, width, width)
            key_out[row : row + TILE, :] = key_tile.astype(BF16)

    fill(padded, rim[...], value_in[...], 0)
    tail_at = level_weight.shape[0] + 1
    head_width = state.shape[1]
    for own in range(group):
        at = own * head_width
        for row in range(0, length, TILE):
            tile = conv_tile(padded, weight, row, at, head_width)
            value_turned[at : at + head_width, row : row + TILE] = tile.T.astype(BF16)
        tail = table[step * group + own, tail_at : tail_at + 1, :]
        state[own] = dot(scaled(value_turned[at : at + head_width, :], tail), key_out[...])


def near_kernel(
    near_count, query_turned, key, value_turned, table, *rest
):
    near, scores = rest[-2:]
    step = pl.program_id(0)
    length = key.shape[0]
    tile_bits = bits_of(TILE)
    sub_bits = bits_of(SUB)

    @pl.when(step == 0)
    def _():
        for at in range(0, length, TILE):
            scores[at : at + TILE, :] = dot(
                key[at : at + TILE, :], query_turned[:, at : at + TILE]
            )

    def row_of(index, start, size):
        return table[0, index : index + 1, start : start + size]

    mid_states = {}
    for level in range(tile_bits + 1, near_count):
        half = 1 << (level - 1)
        for start in range(0, length, 2 * half):
            faded = scaled(value_turned[:, start : start + half], row_of(1 + level, start, half))
            mid_states[level, start] = dot(faded, key[start : start + half, :]).astype(BF16)

    sub_row = lax.broadcasted_iota(jnp.int32, (SUB, TILE), 0)
    sub_lane = lax.broadcasted_iota(jnp.int32, (SUB, TILE), 1)
    inner = sub_lane & (SUB - 1)
    inner_differ = inner ^ sub_row
    inner_causal = inner >= sub_row
    tile_of_lane = sub_lane >> sub_bits
    counts = TILE // SUB
    outer_row = lax.broadcasted_iota(jnp.int32, (counts, TILE), 0)
    outer = lax.broadcasted_iota(jnp.int32, (counts, TILE), 1) >> sub_bits
    outer_differ = outer ^ outer_row
    outer_causal = outer > outer_row

    for at in range(0, length, TILE):
        diagonal = jnp.broadcast_to(row_of(1, at, TILE), (SUB, TILE))
        for level in range(1, sub_bits + 1):
            diagonal = jnp.where(
                inner_differ >= 1 << (level - 1), row_of(1 + level, at, TILE), diagonal
            )
        diagonal = jnp.where(inner_causal, diagonal, 0.0)
        beside = jnp.broadcast_to(row_of(2 + sub_bits, at, TILE), (counts, TILE))
        for level in range(sub_bits + 2, tile_bits + 1):
            beside = jnp.where(
                outer_differ >= 1 << (level - sub_bits - 1), row_of(1 + level, at, TILE), beside
            )
        beside = jnp.where(outer_causal, beside, 0.0)
        mixing = jnp.concatenate(
            [
                jnp.where(
                    tile_of_lane == tile,
                    diagonal,
                    jnp.broadcast_to(beside[tile : tile + 1, :], (SUB, TILE)),
                )
                for tile in range(counts)
            ],
            axis=0,
        )
        left = [scaled(value_turned[:, at : at + TILE], row_of(0, at, TILE))]
        right = [(scores[at : at + TILE, :] * mixing).astype(BF16)]
        for level in range(tile_bits + 1, near_count):
            half = 1 << (level - 1)
            if at & half:
                left.append(mid_states[level, at // (2 * half) * (2 * half)])
                right.append(
                    scaled(query_turned[:, at : at + TILE], row_of(1 + level, at, TILE))
                )
        near[:, at : at + TILE] = dot(
            jnp.concatenate(left, axis=1), jnp.concatenate(right, axis=0)
        ).astype(BF16)


def far_kernel(near_count, query_turned, table, near, gain, digit, lifts, *rest):
    buckets, output = rest[:-1], rest[-1]
    length = query_turned.shape[1]
    group, head_width = buckets[0].shape[:2]
    seq_bits = (len(buckets) + 1) // 2
    upper = digit[0] == 1
    span = 2 * TILE
    for own in range(group):
        at = own * head_width
        parts = [buckets[0][own]]
        for j in range(1, seq_bits):
            mine, other = buckets[2 * j - 1][own], buckets[2 * j][own]
            first = jnp.where(upper, other, mine)
            second = jnp.where(upper, mine, other)
            parts.append(jnp.concatenate([first, second], axis=0))
        states = jnp.concatenate(parts, axis=1)
        head = pl.program_id(0) * group + own
        far_rows = [
            table[own, 1 + near_count + j : 2 + near_count + j, :] * lifts[j, head]
            for j in range(seq_bits)
        ]
        for start in range(0, length, span):
            queries = query_turned[:, start : start + span]
            far = jnp.concatenate(
                [
                    scaled(queries, far_rows[j][:, start : start + span])
                    for j in range(seq_bits)
                ],
                axis=0,
            )
            total = dot(states, far) + near[at : at + head_width, start : start + span].astype(F32)
            power = jnp.mean(total * total, axis=0, keepdims=True)
            normed = total * lax.rsqrt(power + EPSILON)
            output[start : start + span, at : at + head_width] = (
                normed.T * gain[:, at : at + head_width]
            ).astype(BF16)


def whole(shape):
    return pl.BlockSpec(shape, lambda i: (0,) * len(shape))


def exchange(x, bit):
    size = lax.axis_size("seq")
    return lax.ppermute(x, "seq", [(i, i ^ 1 << bit) for i in range(size)])


def climb(state, total, shard_index, seq_bits):
    block = state
    block_total = total
    offset = jnp.zeros_like(total)
    lifts = []
    buckets = []
    for bit in range(seq_bits):
        other = exchange(block.astype(BF16), bit)
        other_total = exchange(block_total, bit)
        digit = shard_index >> bit & 1
        upper = digit == 1
        lifts.append(jnp.where(upper, jnp.exp(offset), 0.0))
        buckets.append(other)
        if bit + 1 < seq_bits:
            share = block.shape[1] // 2
            own_part = lax.dynamic_slice_in_dim(block, digit * share, share, 1)
            other_part = lax.dynamic_slice_in_dim(other, digit * share, share, 1)
            own_scale = jnp.where(upper, 1.0, jnp.exp(other_total))[:, None, None]
            other_scale = jnp.where(upper, jnp.exp(block_total), 1.0)[:, None, None]
            block = own_scale * own_part + other_scale * other_part.astype(F32)
            block_total = block_total + other_total
            offset = offset + jnp.where(upper, other_total, 0.0)
    halves = [buckets[0]]
    for at in range(1, seq_bits):
        bucket = buckets[at]
        for bit in range(at - 1, 0, -1):
            other = exchange(bucket, bit)
            bucket = jnp.where(
                (shard_index >> bit & 1) == 1,
                jnp.concatenate([other, bucket], axis=1),
                jnp.concatenate([bucket, other], axis=1),
            )
        halves += [bucket, exchange(bucket, 0)]
    return jnp.stack(lifts), halves


def on_device(
    query_inputs, key_inputs, value_inputs, log_decay, level_weight, conv_weight, norm_gain
):
    length, width = query_inputs.shape
    channels = value_inputs.shape[1]
    heads = log_decay.shape[0]
    head_width = channels // heads
    taps = conv_weight.shape[0]
    levels = level_weight.shape[0]
    size = lax.axis_size("seq")
    seq_bits = bits_of(size)
    near_count = levels - seq_bits
    shard_index = lax.axis_index("seq")
    rim = jnp.concatenate(
        [x[length - taps + 1 :] for x in (query_inputs, key_inputs, value_inputs)], axis=1
    )
    rim = lax.ppermute(rim, "seq", [(i, i + 1) for i in range(size - 1)])
    total = jnp.sum(log_decay, axis=1)

    group_width = GROUP * head_width
    table_count = levels + 2
    params = pltpu.CompilerParams(vmem_limit_bytes=40 * MIB)
    query_turned, key, value_turned, table, state = pl.pallas_call(
        functools.partial(prepare_kernel, near_count),
        grid=(heads // GROUP,),
        in_specs=[
            whole((length, width)),
            whole((length, width)),
            pl.BlockSpec((length, group_width), lambda i: (0, i)),
            pl.BlockSpec((taps - 1, 2 * width), lambda i: (0, 0)),
            pl.BlockSpec((taps - 1, group_width), lambda i: (0, i + 2 * width // group_width)),
            pl.BlockSpec((taps, 2 * width), lambda i: (0, 0)),
            pl.BlockSpec((taps, group_width), lambda i: (0, i + 2 * width // group_width)),
            whole((heads, length)),
            whole((levels, heads, length)),
        ],
        out_specs=[
            whole((width, length)),
            whole((length, width)),
            pl.BlockSpec((group_width, length), lambda i: (i, 0)),
            whole((heads, table_count, length)),
            pl.BlockSpec((GROUP, head_width, width), lambda i: (i, 0, 0)),
        ],
        out_shape=[
            jax.ShapeDtypeStruct((width, length), BF16),
            jax.ShapeDtypeStruct((length, width), BF16),
            jax.ShapeDtypeStruct((channels, length), BF16),
            jax.ShapeDtypeStruct((heads, table_count, length), F32),
            jax.ShapeDtypeStruct((heads, head_width, width), F32),
        ],
        scratch_shapes=[pltpu.VMEM((SUB + length, max(group_width, 2 * width)), F32)],
        compiler_params=pltpu.CompilerParams(vmem_limit_bytes=60 * MIB),
        name="prepare",
    )(
        query_inputs,
        key_inputs,
        value_inputs,
        rim,
        rim,
        conv_weight,
        conv_weight,
        log_decay,
        level_weight,
    )

    pieces = min(seq_bits, 4)
    piece_heads = heads // pieces
    near = None
    for piece in range(pieces):
        first = piece * piece_heads
        chained = [] if near is None else [near]
        near = pl.pallas_call(
            functools.partial(near_kernel, near_count),
            grid=(piece_heads,),
            in_specs=[
                whole((width, length)),
                whole((length, width)),
                pl.BlockSpec((head_width, length), lambda i, first=first: (i + first, 0)),
                pl.BlockSpec((1, table_count, length), lambda i, first=first: (i + first, 0, 0)),
            ]
            + [pl.BlockSpec(memory_space=pl.ANY)] * len(chained),
            out_specs=pl.BlockSpec((head_width, length), lambda i, first=first: (i + first, 0)),
            out_shape=jax.ShapeDtypeStruct((channels, length), BF16),
            input_output_aliases={4: 0} if chained else {},
            scratch_shapes=[pltpu.VMEM((length, TILE), F32)],
            compiler_params=params,
            cost_estimate=pl.CostEstimate(
                flops=piece_heads * 2 * length * head_width * 8 * TILE * 4,
                bytes_accessed=4 * piece_heads * head_width * length,
                transcendentals=0,
            ),
            name="near",
        )(query_turned, key, value_turned, table, *chained)

    lifts, buckets = climb(state, total, shard_index, seq_bits)
    digit = (shard_index & 1).astype(jnp.int32).reshape(1)
    return pl.pallas_call(
        functools.partial(far_kernel, near_count),
        grid=(heads // GROUP,),
        in_specs=[
            whole((width, length)),
            pl.BlockSpec((GROUP, table_count, length), lambda i: (i, 0, 0)),
            pl.BlockSpec((group_width, length), lambda i: (i, 0)),
            pl.BlockSpec((1, group_width), lambda i: (0, i)),
            pl.BlockSpec(memory_space=pltpu.SMEM),
            pl.BlockSpec(memory_space=pltpu.SMEM),
        ]
        + [pl.BlockSpec((GROUP,) + x.shape[1:], lambda i: (i, 0, 0)) for x in buckets],
        out_specs=pl.BlockSpec((length, group_width), lambda i: (0, i)),
        out_shape=jax.ShapeDtypeStruct((length, channels), BF16),
        compiler_params=params,
        name="far",
    )(query_turned, table, near, norm_gain[None, :], digit, lifts, *buckets)


def solution(mesh):
    return jax.shard_map(
        on_device,
        mesh=mesh,
        in_specs=(
            P(("grp", "seq"), None),
            P(("grp", "seq"), None),
            P(("grp", "seq"), None),
            P(None, ("grp", "seq")),
            P(None, None, ("grp", "seq")),
            P(),
            P(),
        ),
        out_specs=P(("grp", "seq"), None),
        check_vma=False,
    )
```

```python
import functools

import jax
import jax.numpy as jnp
from jax import lax
from jax.experimental import pallas as pl
from jax.experimental.pallas import tpu as pltpu
from jax.sharding import PartitionSpec as P

EPSILON = 1e-05
TILE = 128
SUB = 8
RIM = 16
GROUP = 2
BF16 = jnp.bfloat16
F32 = jnp.float32
MIB = 1024 * 1024


def bits_of(number):
    return number.bit_length() - 1


def dot(a, b):
    return jnp.dot(a, b, preferred_element_type=F32)


def scaled(x, row):
    return x * row.astype(BF16)


def conv_tile(padded, weight, row, column, width):
    taps = weight.shape[0]
    first = SUB - taps + 1 + row
    total = None
    for tap in range(taps):
        term = padded[first + tap : first + tap + TILE, column : column + width] * weight[
            tap : tap + 1, column : column + width
        ]
        total = term if total is None else total + term
    half = total * 0.5
    return half + half * jnp.tanh(half)


def fill(padded, rim, current, column):
    rows, width = current.shape
    padded[0:SUB, column : column + width] = rim.astype(F32)[rim.shape[0] - SUB :]
    padded[SUB : SUB + rows, column : column + width] = current.astype(F32)


def spread(cumul, places, width):
    heads = cumul.shape[0]
    return jnp.concatenate(
        [jnp.broadcast_to(cumul[:, at : at + 1], (heads, width)) for at in places], axis=1
    )


def tables(decay, level_weight, table, length, near_count):
    def put(index, value):
        for head in range(value.shape[0]):
            table[head, index : index + 1, :] = value[head : head + 1, :]

    lane = lax.broadcasted_iota(jnp.int32, decay.shape, 1)
    cumul = decay
    step = 1
    while step < length:
        cumul = cumul + jnp.where(lane >= step, pltpu.roll(cumul, step, 1), 0.0)
        step *= 2
    centre = spread(cumul, [at + TILE // 2 for at in range(0, length, TILE)], TILE)
    rise = jnp.exp(cumul - centre)
    put(0, jnp.exp(centre - cumul))
    tile_bits = bits_of(TILE)
    for level in range(tile_bits + 1):
        put(1 + level, level_weight[level].astype(F32) * rise)
    for level in range(tile_bits + 1, near_count):
        half = 1 << (level - 1)
        edge = spread(cumul, [at + half - 1 for at in range(0, length, 2 * half)], 2 * half)
        gap = cumul - edge
        upper = (lane & half) != 0
        fade = jnp.exp(jnp.where(upper, gap, -gap))
        put(1 + level, jnp.where(upper, level_weight[level].astype(F32), 1.0) * fade)
    fall = jnp.exp(cumul)
    for level in range(near_count, level_weight.shape[0]):
        put(1 + level, level_weight[level].astype(F32) * fall)
    put(1 + level_weight.shape[0], jnp.exp(cumul[:, length - 1 :] - cumul))


def rim_kernel(query_in, key_in, value_in, rim):
    width = query_in.shape[1]
    rim[:, :width] = query_in[...]
    rim[:, width : 2 * width] = key_in[...]
    rim[:, 2 * width :] = value_in[...]


def prepare_kernel(
    near_count,
    query_in,
    key_in,
    value_in,
    rim_first,
    rim,
    weight_first,
    weight,
    decay,
    level_weight,
    query_turned,
    key_out,
    value_turned,
    table,
    state,
    padded,
):
    step = pl.program_id(0)
    length = query_in.shape[0]
    width = query_in.shape[1]
    group = state.shape[0]

    @pl.when(step == 0)
    def _():
        tables(decay[...], level_weight, table, length, near_count)
        fill(padded, rim_first[:, :width], query_in[...], 0)
        fill(padded, rim_first[:, width:], key_in[...], width)
        for row in range(0, length, TILE):
            query_tile = conv_tile(padded, weight_first, row, 0, width)
            query_turned[:, row : row + TILE] = query_tile.astype(BF16).T
            key_tile = conv_tile(padded, weight_first, row, width, width)
            key_out[row : row + TILE, :] = key_tile.astype(BF16)

    fill(padded, rim[...], value_in[...], 0)
    tail_at = level_weight.shape[0] + 1
    head_width = state.shape[1]
    for own in range(group):
        at = own * head_width
        for row in range(0, length, TILE):
            tile = conv_tile(padded, weight, row, at, head_width)
            value_turned[at : at + head_width, row : row + TILE] = tile.astype(BF16).T
        tail = table[step * group + own, tail_at : tail_at + 1, :]
        state[own] = dot(
            scaled(value_turned[at : at + head_width, :], tail), key_out[...]
        ).astype(BF16)


def near_kernel(
    near_count, query_turned, key, value_turned, table, *rest
):
    near, scores = rest[-2:]
    step = pl.program_id(0)
    length = key.shape[0]
    tile_bits = bits_of(TILE)
    sub_bits = bits_of(SUB)

    @pl.when(step == 0)
    def _():
        for at in range(0, length, TILE):
            scores[at : at + TILE, :] = dot(
                key[at : at + TILE, :], query_turned[:, at : at + TILE]
            )

    def row_of(index, start, size):
        return table[0, index : index + 1, start : start + size]

    mid_states = {}
    for level in range(tile_bits + 1, near_count):
        half = 1 << (level - 1)
        for start in range(0, length, 2 * half):
            faded = scaled(value_turned[:, start : start + half], row_of(1 + level, start, half))
            mid_states[level, start] = dot(faded, key[start : start + half, :]).astype(BF16)

    sub_row = lax.broadcasted_iota(jnp.int32, (SUB, TILE), 0)
    sub_lane = lax.broadcasted_iota(jnp.int32, (SUB, TILE), 1)
    inner = sub_lane & (SUB - 1)
    inner_differ = inner ^ sub_row
    inner_causal = inner >= sub_row
    tile_of_lane = sub_lane >> sub_bits
    counts = TILE // SUB
    outer_row = lax.broadcasted_iota(jnp.int32, (counts, TILE), 0)
    outer = lax.broadcasted_iota(jnp.int32, (counts, TILE), 1) >> sub_bits
    outer_differ = outer ^ outer_row
    outer_causal = outer > outer_row

    for at in range(0, length, TILE):
        diagonal = jnp.broadcast_to(row_of(1, at, TILE), (SUB, TILE))
        for level in range(1, sub_bits + 1):
            diagonal = jnp.where(
                inner_differ >= 1 << (level - 1), row_of(1 + level, at, TILE), diagonal
            )
        diagonal = jnp.where(inner_causal, diagonal, 0.0)
        beside = jnp.broadcast_to(row_of(2 + sub_bits, at, TILE), (counts, TILE))
        for level in range(sub_bits + 2, tile_bits + 1):
            beside = jnp.where(
                outer_differ >= 1 << (level - sub_bits - 1), row_of(1 + level, at, TILE), beside
            )
        beside = jnp.where(outer_causal, beside, 0.0)
        mixing = jnp.concatenate(
            [
                jnp.where(
                    tile_of_lane == tile,
                    diagonal,
                    jnp.broadcast_to(beside[tile : tile + 1, :], (SUB, TILE)),
                )
                for tile in range(counts)
            ],
            axis=0,
        )
        left = [scaled(value_turned[:, at : at + TILE], row_of(0, at, TILE))]
        right = [(scores[at : at + TILE, :] * mixing).astype(BF16)]
        for level in range(tile_bits + 1, near_count):
            half = 1 << (level - 1)
            if at & half:
                left.append(mid_states[level, at // (2 * half) * (2 * half)])
                right.append(
                    scaled(query_turned[:, at : at + TILE], row_of(1 + level, at, TILE))
                )
        near[:, at : at + TILE] = dot(
            jnp.concatenate(left, axis=1), jnp.concatenate(right, axis=0)
        ).astype(BF16)


def far_kernel(near_count, query_turned, table, near, gain, digit, lifts, *rest):
    buckets, output = rest[:-1], rest[-1]
    length = query_turned.shape[1]
    group, head_width = buckets[0].shape[:2]
    seq_bits = (len(buckets) + 1) // 2
    upper = digit[0] == 1
    span = 2 * TILE
    for own in range(group):
        at = own * head_width
        parts = [buckets[0][own]]
        for j in range(1, seq_bits):
            mine, other = buckets[2 * j - 1][own], buckets[2 * j][own]
            first = jnp.where(upper, other, mine)
            second = jnp.where(upper, mine, other)
            parts.append(jnp.concatenate([first, second], axis=0))
        states = jnp.concatenate(parts, axis=1)
        gains = jnp.broadcast_to(gain[:, at : at + head_width], (head_width, head_width)).T
        gains = jnp.concatenate([gains] * (span // head_width), axis=1)
        head = pl.program_id(0) * group + own
        far_rows = [
            table[own, 1 + near_count + j : 2 + near_count + j, :] * lifts[j, head]
            for j in range(seq_bits)
        ]
        for start in range(0, length, span):
            queries = query_turned[:, start : start + span]
            far = jnp.concatenate(
                [
                    scaled(queries, far_rows[j][:, start : start + span])
                    for j in range(seq_bits)
                ],
                axis=0,
            )
            total = dot(states, far) + near[at : at + head_width, start : start + span].astype(F32)
            power = jnp.mean(total * total, axis=0, keepdims=True)
            normed = total * lax.rsqrt(power + EPSILON) * gains
            output[start : start + span, at : at + head_width] = normed.astype(BF16).T


def whole(shape):
    return pl.BlockSpec(shape, lambda i: (0,) * len(shape))


def exchange(x, bit):
    size = lax.axis_size("seq")
    return lax.ppermute(x, "seq", [(i, i ^ 1 << bit) for i in range(size)])


def climb(state, total, shard_index, seq_bits, beside):
    block = state
    block_total = total
    offset = jnp.zeros_like(total)
    near = None
    lifts = []
    buckets = []
    for bit in range(seq_bits):
        other = exchange(block.astype(BF16), bit)
        other_total = exchange(block_total, bit)
        near = beside(bit, near)
        other, near = lax.optimization_barrier((other, near))
        digit = shard_index >> bit & 1
        upper = digit == 1
        lifts.append(jnp.where(upper, jnp.exp(offset), 0.0))
        buckets.append(other)
        if bit + 1 < seq_bits:
            share = block.shape[1] // 2
            own_part = lax.dynamic_slice_in_dim(block, digit * share, share, 1)
            other_part = lax.dynamic_slice_in_dim(other, digit * share, share, 1)
            own_scale = jnp.where(upper, 1.0, jnp.exp(other_total))[:, None, None]
            other_scale = jnp.where(upper, jnp.exp(block_total), 1.0)[:, None, None]
            block = own_scale * own_part.astype(F32) + other_scale * other_part.astype(F32)
            block_total = block_total + other_total
            offset = offset + jnp.where(upper, other_total, 0.0)
    halves = [buckets[0]]
    for at in range(1, seq_bits):
        bucket = buckets[at]
        for bit in range(at - 1, 0, -1):
            other = exchange(bucket, bit)
            bucket = jnp.where(
                (shard_index >> bit & 1) == 1,
                jnp.concatenate([other, bucket], axis=1),
                jnp.concatenate([bucket, other], axis=1),
            )
        halves += [bucket, exchange(bucket, 0)]
    return jnp.stack(lifts), halves, near


def on_device(
    query_inputs, key_inputs, value_inputs, log_decay, level_weight, conv_weight, norm_gain
):
    length, width = query_inputs.shape
    channels = value_inputs.shape[1]
    heads = log_decay.shape[0]
    head_width = channels // heads
    taps = conv_weight.shape[0]
    levels = level_weight.shape[0]
    size = lax.axis_size("seq")
    seq_bits = bits_of(size)
    near_count = levels - seq_bits
    shard_index = lax.axis_index("seq")
    last = length // RIM - 1
    rim = pl.pallas_call(
        rim_kernel,
        grid=(1,),
        in_specs=[
            pl.BlockSpec((RIM, columns), lambda i: (last, 0)) for columns in (width, width, channels)
        ],
        out_specs=whole((RIM, 2 * width + channels)),
        out_shape=jax.ShapeDtypeStruct((RIM, 2 * width + channels), BF16),
        compiler_params=pltpu.CompilerParams(vmem_limit_bytes=60 * MIB),
        name="rim",
    )(query_inputs, key_inputs, value_inputs)
    rim = lax.ppermute(rim, "seq", [(i, i + 1) for i in range(size - 1)])
    total = jnp.sum(log_decay, axis=1)

    group_width = GROUP * head_width
    table_count = levels + 2
    params = pltpu.CompilerParams(vmem_limit_bytes=60 * MIB)
    query_turned, key, value_turned, table, state = pl.pallas_call(
        functools.partial(prepare_kernel, near_count),
        grid=(heads // GROUP,),
        in_specs=[
            whole((length, width)),
            whole((length, width)),
            pl.BlockSpec((length, group_width), lambda i: (0, i)),
            pl.BlockSpec((RIM, 2 * width), lambda i: (0, 0)),
            pl.BlockSpec((RIM, group_width), lambda i: (0, i + 2 * width // group_width)),
            pl.BlockSpec((taps, 2 * width), lambda i: (0, 0)),
            pl.BlockSpec((taps, group_width), lambda i: (0, i + 2 * width // group_width)),
            whole((heads, length)),
            whole((levels, heads, length)),
        ],
        out_specs=[
            whole((width, length)),
            whole((length, width)),
            pl.BlockSpec((group_width, length), lambda i: (i, 0)),
            whole((heads, table_count, length)),
            pl.BlockSpec((GROUP, head_width, width), lambda i: (i, 0, 0)),
        ],
        out_shape=[
            jax.ShapeDtypeStruct((width, length), BF16),
            jax.ShapeDtypeStruct((length, width), BF16),
            jax.ShapeDtypeStruct((channels, length), BF16),
            jax.ShapeDtypeStruct((heads, table_count, length), F32),
            jax.ShapeDtypeStruct((heads, head_width, width), BF16),
        ],
        scratch_shapes=[pltpu.VMEM((SUB + length, max(group_width, 2 * width)), F32)],
        compiler_params=pltpu.CompilerParams(vmem_limit_bytes=60 * MIB),
        name="prepare",
    )(
        query_inputs,
        key_inputs,
        value_inputs,
        rim,
        rim,
        conv_weight,
        conv_weight,
        log_decay,
        level_weight,
    )

    pieces = min(seq_bits, 4)
    piece_heads = heads // pieces

    def near_piece(piece, near):
        if piece >= pieces:
            return near
        first = piece * piece_heads
        chained = [] if near is None else [near]
        return pl.pallas_call(
            functools.partial(near_kernel, near_count),
            grid=(piece_heads,),
            in_specs=[
                whole((width, length)),
                whole((length, width)),
                pl.BlockSpec((head_width, length), lambda i, first=first: (i + first, 0)),
                pl.BlockSpec((1, table_count, length), lambda i, first=first: (i + first, 0, 0)),
            ]
            + [pl.BlockSpec(memory_space=pl.ANY)] * len(chained),
            out_specs=pl.BlockSpec((head_width, length), lambda i, first=first: (i + first, 0)),
            out_shape=jax.ShapeDtypeStruct((channels, length), BF16),
            input_output_aliases={4: 0} if chained else {},
            scratch_shapes=[pltpu.VMEM((length, TILE), F32)],
            compiler_params=params,
            cost_estimate=pl.CostEstimate(
                flops=piece_heads * 2 * length * head_width * 8 * TILE * 4,
                bytes_accessed=4 * piece_heads * head_width * length,
                transcendentals=0,
            ),
            name="near",
        )(query_turned, key, value_turned, table, *chained)

    lifts, buckets, near = climb(state, total, shard_index, seq_bits, near_piece)
    digit = (shard_index & 1).astype(jnp.int32).reshape(1)
    return pl.pallas_call(
        functools.partial(far_kernel, near_count),
        grid=(heads // GROUP,),
        in_specs=[
            whole((width, length)),
            pl.BlockSpec((GROUP, table_count, length), lambda i: (i, 0, 0)),
            pl.BlockSpec((group_width, length), lambda i: (i, 0)),
            pl.BlockSpec((1, group_width), lambda i: (0, i)),
            pl.BlockSpec(memory_space=pltpu.SMEM),
            pl.BlockSpec(memory_space=pltpu.SMEM),
        ]
        + [pl.BlockSpec((GROUP,) + x.shape[1:], lambda i: (i, 0, 0)) for x in buckets],
        out_specs=pl.BlockSpec((length, group_width), lambda i: (0, i)),
        out_shape=jax.ShapeDtypeStruct((length, channels), BF16),
        compiler_params=params,
        name="far",
    )(query_turned, table, near, norm_gain[None, :], digit, lifts, *buckets)


def solution(mesh):
    return jax.shard_map(
        on_device,
        mesh=mesh,
        in_specs=(
            P(("grp", "seq"), None),
            P(("grp", "seq"), None),
            P(("grp", "seq"), None),
            P(None, ("grp", "seq")),
            P(None, None, ("grp", "seq")),
            P(),
            P(),
        ),
        out_specs=P(("grp", "seq"), None),
        check_vma=False,
    )
```
